32 devices in a mesh: frame: 16 (over z, y, x), strip: 2 (over core).
Axes of the slice: x: 2, y: 2, z: 4, core: 2. Of those that a mesh axis runs over, the one named last changes fastest.
Arguments:
- saved_qkv: bfloat16 [128, 96, 3456], P('frame', 'strip'), may hold values from -6 to 6
- cotangent: bfloat16 [128, 96, 1152], P('frame', 'strip'), may hold values from -6 to 6
- out_weight: bfloat16 [1152, 1152], P('frame', 'strip'), may hold values from -0.1875 to 0.1875
- qkv_weight: bfloat16 [3, 1152, 1152], P(None, 'frame', 'strip'), may hold values from -0.1875 to 0.1875
- offsets: int32 [128], replicated, may hold values from 0 to 191, as said below
- sink_frame: int32 [1], replicated, may hold values from 0 to 64
- window: int32 [1], replicated, may hold values from 32 to 64
Outputs:
- grad_input: bfloat16 [128, 96, 1152], P('frame', 'strip')
The draws below stay inside these ranges and needn't reach their ends.
Inputs may be any that keep to these rules, and one draw needn't show every extreme that they name: offsets start at 0 and rise by 1 or 2 from each frame to the next.
All inputs are finite; a program needn't handle non-finite values.
Results may differ from the reference program's by a relative error of at most 0.0071.
Values may be sent and summed in bfloat16 or wider, within the bound.
A program may use at most 64 MiB of HBM per device.

```python
import math
import jax
import jax.numpy as jnp
from jax import lax

D = 1152
H = 16
HD = 72
S_DEV = 48
F = 128
S = 96


def draw_offsets(key, part):
    order = jax.random.permutation(jax.random.fold_in(key, 5), F - 1)
    steps_drawn = jnp.where(order < F // 2, 2, 1).astype(jnp.int32)
    summed = jnp.concatenate([jnp.zeros((1,), jnp.int32), jnp.cumsum(steps_drawn).astype(jnp.int32)])
    return summed.astype(jnp.int32)


def draw_saved_qkv(key, part):
    keys_all = jax.random.split(jax.random.fold_in(key, 11), 6)
    result = jnp.clip(jax.random.normal(keys_all[5], (F, S, 3 * D), jnp.float32), -6.0, 6.0)
    return result.astype(jnp.bfloat16)


def block_scale(own_key, dims, cuts, smallest, high):
    level, own = 1.0, jax.random.fold_in(own_key, 6)
    for dim, blocks in cuts:
        draws = jnp.exp(jax.random.uniform(jax.random.fold_in(own, dim), (blocks,), jnp.float32, smallest / len(cuts), high / len(cuts)))
        level = level * jnp.repeat(draws, dims[dim] // blocks).reshape([-1 if axis == dim else 1 for axis in range(len(dims))])
    return level


def bell_draw(key, extent, scale, most, cuts=(), held_as=jnp.bfloat16):
    values = scale * jax.random.normal(key, extent, jnp.float32)
    if cuts:
        values = values * block_scale(key, extent, cuts, -0.22, 0.18)
    return jnp.clip(values, -most, most).astype(held_as)


def setup_inputs(seed: int = 0) -> dict:
    keys = jax.random.split(jax.random.key(seed), 8)
    return {
        "saved_qkv": draw_saved_qkv(jax.random.fold_in(keys[7], 71), 0),
        "cotangent": bell_draw(keys[1], (F, S, D), 1.0, 6.0, ((0, 16), (1, 2))),
        "out_weight": bell_draw(keys[2], (D, D), D ** -0.5, 0.1875, ((0, 16), (1, 2))),
        "qkv_weight": bell_draw(keys[3], (3, D, D), D ** -0.5, 0.1875, ((1, 16), (2, 2))),
        "offsets": draw_offsets(jax.random.fold_in(keys[7], 71), 0),
        "sink_frame": jax.random.randint(keys[5], (1,), 0, F // 2 + 1).astype(jnp.int32),
        "window": jax.random.randint(keys[6], (1,), F // 4, F // 2 + 1).astype(jnp.int32),
    }


def visibility(offsets, sink_frame, window):
    frame_ids = jnp.arange(offsets.shape[0], dtype=jnp.int32)
    time_gap = offsets[:, None] - offsets[None, :]
    in_window = time_gap < window[0]
    anchor = frame_ids[None, :] == sink_frame[0]
    return (time_gap >= 0) & (in_window | anchor)

def attention_grads(block_qkv, upstream, visible, factor):
    frames, places, _ = block_qkv.shape
    queries = block_qkv[:, :, :D].reshape(frames, places, H, HD).astype(jnp.float32)
    key_rows = block_qkv[:, :, D:2 * D].reshape(frames, places, H, HD).astype(jnp.float32)
    values = block_qkv[:, :, 2 * D:].reshape(frames, places, H, HD).astype(jnp.float32)
    grad_up = upstream.reshape(frames, places, H, HD).astype(jnp.float32)
    scores = jnp.einsum('iphd,jphd->phij', queries, key_rows) * factor
    masked = jnp.where(visible, scores, -jnp.inf)
    row_top = lax.optimization_barrier(jnp.max(masked, axis=-1, keepdims=True))
    raised = jnp.exp(masked - row_top)
    probs = raised / lax.optimization_barrier(jnp.sum(raised, axis=-1, keepdims=True))
    probs_low = probs.astype(jnp.bfloat16).astype(jnp.float32)
    grad_p = jnp.einsum('iphd,jphd->phij', grad_up, values)
    row_sum = lax.optimization_barrier(jnp.sum(probs * grad_p, axis=-1, keepdims=True))
    grad_s = (probs * (grad_p - row_sum)).astype(jnp.bfloat16).astype(jnp.float32)
    grad_v = jnp.einsum('phij,iphd->jphd', probs_low, grad_up).astype(jnp.bfloat16)
    grad_q = (jnp.einsum('phij,jphd->iphd', grad_s, key_rows) * factor).astype(jnp.bfloat16)
    grad_k = (jnp.einsum('phij,iphd->jphd', grad_s, queries) * factor).astype(jnp.bfloat16)
    return jnp.concatenate([grad_q.reshape(frames, places, D), grad_k.reshape(frames, places, D), grad_v.reshape(frames, places, D)], axis=2)

def reference(saved_qkv, cotangent, out_weight, qkv_weight, offsets, sink_frame, window):
    visible = visibility(offsets, sink_frame, window)
    factor = 1.0 / math.sqrt(HD)
    weight_float = qkv_weight.astype(jnp.float32)

    def one_block(block_index):
        first_row = block_index * S_DEV
        block_qkv = lax.dynamic_slice_in_dim(saved_qkv, first_row, S_DEV, 1)
        block_cot = lax.dynamic_slice_in_dim(cotangent, first_row, S_DEV, 1)
        flattened = block_cot.reshape(F * S_DEV, D)
        upstream = jnp.dot(flattened, out_weight.T, preferred_element_type=jnp.float32).astype(jnp.bfloat16)
        upstream = upstream.reshape(F, S_DEV, D)
        grads = attention_grads(block_qkv, upstream, visible, factor)
        stacked = grads.reshape(F * S_DEV, 3, D).astype(jnp.float32)
        total = jnp.einsum('tcd,crd->tr', stacked, weight_float)
        return total.astype(jnp.bfloat16).reshape(F, S_DEV, D)
    blocks = lax.map(one_block, jnp.arange(S // S_DEV, dtype=jnp.int32))
    return jnp.transpose(blocks, (1, 0, 2, 3)).reshape(F, S, D)
```

```python
import functools
import math

import jax
import jax.numpy as jnp
from jax import lax
from jax.experimental import pallas as pl
from jax.experimental.pallas import tpu as pltpu
from jax.sharding import PartitionSpec as P

D = 1152
H = 16
HD = 72
LANES = 128
MESH = pl.DeviceIdType.MESH
VMEM_SPEC = pl.BlockSpec(memory_space=pltpu.VMEM)


def visibility(offsets, sink_frame, window):
    frame_ids = jnp.arange(offsets.shape[0], dtype=jnp.int32)
    time_gap = offsets[:, None] - offsets[None, :]
    in_window = time_gap < window[0]
    anchor = frame_ids[None, :] == sink_frame[0]
    return (time_gap >= 0) & (in_window | anchor)


def enter(n):
    me = lax.axis_index("frame")
    strip = lax.axis_index("strip")
    barrier = pltpu.get_barrier_semaphore()

    @pl.loop(1, n)
    def _(d):
        pl.semaphore_signal(
            barrier, inc=1, device_id=(lax.rem(me + d, n), strip), device_id_type=MESH
        )

    pl.semaphore_wait(barrier, n - 1)
    return me, strip


def spread_kernel(n, spots, send_ref, recv_ref, own_sem, send_sem, recv_sem):
    me, strip = enter(n)

    def copy(j, d):
        to = lax.rem(me + d, n)
        return pltpu.make_async_remote_copy(
            src_ref=send_ref.at[to * spots + j],
            dst_ref=recv_ref.at[j, me],
            send_sem=send_sem.at[j, d],
            recv_sem=recv_sem.at[j, d],
            device_id=(to, strip),
            device_id_type=MESH,
        )

    for j in range(spots):

        @pl.loop(1, n)
        def _(d):
            copy(j, d).start()

    for j in range(spots):
        own = pltpu.make_async_copy(send_ref.at[me * spots + j], recv_ref.at[j, me], own_sem.at[j])
        own.start()
        own.wait()
    for j in range(spots):

        @pl.loop(1, n)
        def _(d):
            copy(j, d).wait()


def nt_dot(a, b):
    return lax.dot_general(a, b, (((1,), (1,)), ((), ())), preferred_element_type=jnp.float32)


def head_columns(h):
    low = h * HD // LANES * LANES
    high = -(-(h * HD + HD) // LANES) * LANES
    return low, high


def heads_gradients(x_ref, grad_out, bias, grads):
    factor = 1.0 / math.sqrt(HD)
    frames = bias.shape[0]
    grads[...] = jnp.zeros_like(grads)
    for h in range(H):
        low, high = head_columns(h)
        feature = lax.broadcasted_iota(jnp.int32, (frames, high - low), 1) + low
        own = (feature >= h * HD) & (feature < h * HD + HD)
        zero = jnp.zeros((frames, high - low), jnp.bfloat16)
        q = jnp.where(own, x_ref[:, low:high], zero)
        k_all = x_ref[:, D + low : D + high]
        k = jnp.where(own, k_all, zero)
        v_all = x_ref[:, 2 * D + low : 2 * D + high]
        g = jnp.where(own, grad_out[:, low:high], zero)
        masked = nt_dot(q, k_all) * factor + bias
        raised = jnp.exp(masked - jnp.max(masked, axis=1, keepdims=True))
        probs = raised * (1.0 / jnp.sum(raised, axis=1, keepdims=True))
        grad_p = nt_dot(g, v_all)
        row_sum = jnp.sum(probs * grad_p, axis=1, keepdims=True)
        grad_s = probs * (grad_p - row_sum)
        grad_s_t = grad_s.T.astype(jnp.bfloat16)
        grad_s = grad_s.astype(jnp.bfloat16)
        probs_t = probs.T.astype(jnp.bfloat16)
        grads[:, low:high] += jnp.dot(grad_s, k, preferred_element_type=jnp.float32) * factor
        grads[:, D + low : D + high] += (
            jnp.dot(grad_s_t, q, preferred_element_type=jnp.float32) * factor
        )
        grads[:, 2 * D + low : 2 * D + high] += jnp.dot(
            probs_t, g, preferred_element_type=jnp.float32
        )


def attend_kernel(
    n, spots, x_ref, wo_ref, wqkv_ref, bias_ref, ret_ref,
    xs, grad_out, grads, outs, own_sem, send_sem, recv_sem,
):
    me, strip = enter(n)
    frames = bias_ref.shape[0]

    def copy(j, d):
        to = lax.rem(me + d, n)
        return pltpu.make_async_remote_copy(
            src_ref=outs.at[j, to],
            dst_ref=ret_ref.at[me * spots + j],
            send_sem=send_sem.at[j, d],
            recv_sem=recv_sem.at[j, d],
            device_id=(to, strip),
            device_id_type=MESH,
        )

    def own_copy(j):
        return pltpu.make_async_copy(outs.at[j, me], ret_ref.at[me * spots + j], own_sem.at[j])

    @pl.loop(0, spots)
    def _(j):
        x = x_ref[j].astype(jnp.float32).reshape(frames, 4 * D).astype(jnp.bfloat16)
        xs[...] = x[:, : 3 * D]
        grad_out[...] = nt_dot(x[:, 3 * D :], wo_ref[...]).astype(jnp.bfloat16)
        heads_gradients(xs, grad_out, bias_ref[...], grads)
        total = nt_dot(grads[:, :D].astype(jnp.bfloat16), wqkv_ref[0])
        total += nt_dot(grads[:, D : 2 * D].astype(jnp.bfloat16), wqkv_ref[1])
        total += nt_dot(grads[:, 2 * D :].astype(jnp.bfloat16), wqkv_ref[2])
        outs[j] = total.reshape(n, frames // n, D).astype(jnp.bfloat16)

        @pl.loop(1, n)
        def _(d):
            copy(j, d).start()

        own_copy(j).start()

    @pl.loop(0, spots)
    def _(j):
        own_copy(j).wait()

        @pl.loop(1, n)
        def _(d):
            copy(j, d).wait()


def per_device(n, saved_qkv, cotangent, out_weight, qkv_weight, offsets, sink_frame, window):
    frames_dev, strip_len, _ = cotangent.shape
    frames, spots = frames_dev * n, strip_len // n
    wo = lax.all_gather(out_weight, "frame", axis=0, tiled=True)
    wo = lax.all_gather(wo, "strip", axis=1, tiled=True)
    wqkv = lax.all_gather(qkv_weight, "frame", axis=1, tiled=True)
    wqkv = lax.all_gather(wqkv, "strip", axis=2, tiled=True)
    send = jnp.concatenate([saved_qkv, cotangent], axis=2).transpose(1, 0, 2)
    bias = jnp.where(visibility(offsets, sink_frame, window), 0.0, -jnp.inf).astype(jnp.float32)
    sems = [
        pltpu.SemaphoreType.DMA((spots,)),
        pltpu.SemaphoreType.DMA((spots, n)),
        pltpu.SemaphoreType.DMA((spots, n)),
    ]
    moved = pl.pallas_call(
        functools.partial(spread_kernel, n, spots),
        out_shape=jax.ShapeDtypeStruct((spots, n, frames_dev, 4 * D), jnp.bfloat16),
        in_specs=[VMEM_SPEC],
        out_specs=VMEM_SPEC,
        scratch_shapes=sems,
        compiler_params=pltpu.CompilerParams(
            collective_id=0, has_side_effects=True, vmem_limit_bytes=24 << 20
        ),
        cost_estimate=pl.CostEstimate(flops=0, bytes_accessed=300 << 20, transcendentals=0),
        name="spread",
    )(send)
    returned = pl.pallas_call(
        functools.partial(attend_kernel, n, spots),
        out_shape=jax.ShapeDtypeStruct((strip_len, frames_dev, D), jnp.bfloat16),
        in_specs=[VMEM_SPEC] * 4,
        out_specs=VMEM_SPEC,
        scratch_shapes=[
            pltpu.VMEM((frames, 3 * D), jnp.bfloat16),
            pltpu.VMEM((frames, D), jnp.bfloat16),
            pltpu.VMEM((frames, 3 * D), jnp.float32),
            pltpu.VMEM((spots, n, frames_dev, D), jnp.bfloat16),
        ]
        + sems,
        compiler_params=pltpu.CompilerParams(
            collective_id=1, has_side_effects=True, vmem_limit_bytes=48 << 20
        ),
        name="attend",
    )(moved, wo, wqkv, bias)
    return returned.transpose(1, 0, 2)


def solution(mesh):
    placed = (
        P("frame", "strip", None),
        P("frame", "strip", None),
        P("frame", "strip"),
        P(None, "frame", "strip"),
        P(),
        P(),
        P(),
    )
    return jax.shard_map(
        functools.partial(per_device, mesh.shape["frame"]),
        mesh=mesh,
        in_specs=placed,
        out_specs=P("frame", "strip", None),
        check_vma=False,
    )
```

```python
import functools
import math

import jax
import jax.numpy as jnp
from jax import lax
from jax.experimental import pallas as pl
from jax.experimental.pallas import tpu as pltpu
from jax.sharding import PartitionSpec as P

D = 1152
H = 16
HD = 72
LANES = 128
MESH = pl.DeviceIdType.MESH
VMEM_SPEC = pl.BlockSpec(memory_space=pltpu.VMEM)


def visibility(offsets, sink_frame, window):
    frame_ids = jnp.arange(offsets.shape[0], dtype=jnp.int32)
    time_gap = offsets[:, None] - offsets[None, :]
    in_window = time_gap < window[0]
    anchor = frame_ids[None, :] == sink_frame[0]
    return (time_gap >= 0) & (in_window | anchor)


def remote(src, dst, send_sem, recv_sem, to):
    return pltpu.make_async_remote_copy(
        src_ref=src, dst_ref=dst, send_sem=send_sem, recv_sem=recv_sem,
        device_id=to, device_id_type=MESH,
    )


def nt_dot(a, b):
    return lax.dot_general(a, b, (((1,), (1,)), ((), ())), preferred_element_type=jnp.float32)


def head_columns(h):
    low = h * HD // LANES * LANES
    high = -(-(h * HD + HD) // LANES) * LANES
    return low, high


def heads_gradients(x_ref, grad_out, bias, grads):
    factor = 1.0 / math.sqrt(HD)
    frames = bias.shape[0]
    grads[...] = jnp.zeros_like(grads)
    for h in range(H):
        low, high = head_columns(h)
        feature = lax.broadcasted_iota(jnp.int32, (frames, high - low), 1) + low
        own = (feature >= h * HD) & (feature < h * HD + HD)
        zero = jnp.zeros((frames, high - low), jnp.bfloat16)
        q = jnp.where(own, x_ref[:, low:high], zero)
        k_all = x_ref[:, D + low : D + high]
        k = jnp.where(own, k_all, zero)
        v_all = x_ref[:, 2 * D + low : 2 * D + high]
        g = jnp.where(own, grad_out[:, low:high], zero)
        masked = nt_dot(q, k_all) * factor + bias
        raised = jnp.exp(masked - jnp.max(masked, axis=1, keepdims=True))
        probs = raised * (1.0 / jnp.sum(raised, axis=1, keepdims=True))
        grad_p = nt_dot(g, v_all)
        row_sum = jnp.sum(probs * grad_p, axis=1, keepdims=True)
        grad_s = probs * (grad_p - row_sum)
        grad_s_t = grad_s.T.astype(jnp.bfloat16)
        grad_s = grad_s.astype(jnp.bfloat16)
        probs_t = probs.T.astype(jnp.bfloat16)
        grads[:, low:high] += jnp.dot(grad_s, k, preferred_element_type=jnp.float32) * factor
        grads[:, D + low : D + high] += (
            jnp.dot(grad_s_t, q, preferred_element_type=jnp.float32) * factor
        )
        grads[:, 2 * D + low : 2 * D + high] += jnp.dot(
            probs_t, g, preferred_element_type=jnp.float32
        )


def block_kernel(
    n, strips, spots, send_ref, local_ref, bias_ref, ret_ref,
    recv, pieces, weights, xs, grad_out, grads, outs,
    own_sem, piece_send, piece_recv, z_send, z_recv, y_send, y_recv,
    x_send, x_recv, mine_send, mine_recv, other_send, other_recv,
    in_send, in_recv, out_send, out_recv,
):
    frames = bias_ref.shape[0]
    lines = n // 4
    me, strip = lax.axis_index("frame"), lax.axis_index("strip")
    half, x, y, z = strip // (strips // 2), lax.rem(me, 2), lax.rem(me // 2, 2), me // 4
    twin = lax.rem(strip + strips // 2, strips)
    beside = me + 1 - 2 * x
    matrix = 2 * half + x

    barrier = pltpu.get_barrier_semaphore()

    @pl.loop(1, n)
    def _(d):
        pl.semaphore_signal(
            barrier, inc=1, device_id=(lax.rem(me + d, n), strip), device_id_type=MESH
        )

    for to in ((me, twin), (beside, twin)):
        pl.semaphore_signal(barrier, inc=1, device_id=to, device_id_type=MESH)
    pl.semaphore_wait(barrier, n + 1)

    def piece(k):
        to_x, to_half = lax.rem(x + k // 2, 2), lax.rem(half + k % 2, 2)
        return remote(
            local_ref.at[2 * to_half + to_x], pieces.at[x, half],
            piece_send.at[k], piece_recv.at[k],
            (beside if k // 2 else me, twin if k % 2 else strip),
        )

    for k in (1, 2, 3):
        piece(k).start()
    own = pltpu.make_async_copy(local_ref.at[matrix], pieces.at[x, half], own_sem.at[0])
    own.start()

    def inward(j, d):
        to = lax.rem(me + d, n)
        return remote(
            send_ref.at[to * spots + j], recv.at[j, me],
            in_send.at[j, d], in_recv.at[j, d], (to, strip),
        )

    def own_inward(j):
        return pltpu.make_async_copy(
            send_ref.at[me * spots + j], recv.at[j, me], own_sem.at[1 + j]
        )

    def start_inward(j):
        @pl.loop(1, n)
        def _(d):
            inward(j, d).start()

        own_inward(j).start()

    start_inward(0)
    own.wait()
    for k in (1, 2, 3):
        piece(k).wait()
    rows = [
        jnp.concatenate([pieces[i, c].astype(jnp.float32) for c in range(2)], axis=1)
        for i in range(2)
    ]
    weights[matrix, 2 * z + y] = jnp.concatenate(rows, axis=0).astype(jnp.bfloat16)

    def block_at(k):
        return 2 * lax.rem(z + lines - k % lines, lines) + lax.rem(y + k // lines, 2)

    def along_z(d):
        to = 4 * lax.rem(z + d, lines) + lax.rem(me, 4)
        ref = weights.at[matrix, 2 * z + y]
        return remote(ref, ref, z_send.at[d], z_recv.at[d], (to, strip))

    def across_y(k):
        ref = weights.at[matrix, block_at(k)]
        return remote(ref, ref, y_send.at[k], y_recv.at[k], (me + 2 - 4 * y, strip))

    def across_x(k):
        ref = weights.at[matrix, block_at(k)]
        return remote(ref, ref, x_send.at[k], x_recv.at[k], (beside, strip))

    def mine_to_twin(k):
        ref = weights.at[matrix, block_at(k)]
        return remote(ref, ref, mine_send.at[k], mine_recv.at[k], (me, twin))

    def other_to_twin(k):
        ref = weights.at[2 * half + 1 - x, block_at(k)]
        return remote(ref, ref, other_send.at[k], other_recv.at[k], (me, twin))

    @pl.loop(1, lines)
    def _(d):
        along_z(d).start()

    across_y(0).start()
    across_x(0).start()
    mine_to_twin(0).start()
    start_inward(1)

    @pl.loop(1, lines)
    def _(k):
        along_z(k).wait_recv()
        across_y(k).start()
        across_x(k).start()
        mine_to_twin(k).start()

    @pl.loop(0, lines)
    def _(k):
        across_y(k).wait_recv()
        across_x(k + lines).start()
        mine_to_twin(k + lines).start()

    for j in range(2, spots):
        start_inward(j)

    @pl.loop(0, 2 * lines)
    def _(k):
        across_x(k).wait_recv()
        other_to_twin(k).start()

    @pl.loop(0, 2 * lines)
    def _(k):
        mine_to_twin(k).wait()
        other_to_twin(k).wait()
        across_x(k).wait_send()

    @pl.loop(1, lines)
    def _(d):
        along_z(d).wait_send()

    @pl.loop(0, lines)
    def _(k):
        across_y(k).wait_send()

    def outward(j, d):
        to = lax.rem(me + d, n)
        return remote(
            outs.at[j, to], ret_ref.at[me * spots + j],
            out_send.at[j, d], out_recv.at[j, d], (to, strip),
        )

    def own_outward(j):
        return pltpu.make_async_copy(
            outs.at[j, me], ret_ref.at[me * spots + j], own_sem.at[1 + spots + j]
        )

    def whole(m):
        return weights[m].reshape(D, D)

    @pl.loop(0, spots)
    def _(j):
        own_inward(j).wait()

        @pl.loop(1, n)
        def _(d):
            inward(j, d).wait()

        moved = recv[j].astype(jnp.float32).reshape(frames, 4 * D).astype(jnp.bfloat16)
        xs[...] = moved[:, : 3 * D]
        grad_out[...] = nt_dot(moved[:, 3 * D :], whole(0)).astype(jnp.bfloat16)
        heads_gradients(xs, grad_out, bias_ref[...], grads)
        total = nt_dot(grads[:, :D].astype(jnp.bfloat16), whole(1))
        total += nt_dot(grads[:, D : 2 * D].astype(jnp.bfloat16), whole(2))
        total += nt_dot(grads[:, 2 * D :].astype(jnp.bfloat16), whole(3))
        outs[j] = total.reshape(n, frames // n, D).astype(jnp.bfloat16)

        @pl.loop(1, n)
        def _(d):
            outward(j, d).start()

        own_outward(j).start()

    @pl.loop(0, spots)
    def _(j):
        own_outward(j).wait()

        @pl.loop(1, n)
        def _(d):
            outward(j, d).wait()


def per_device(n, strips, saved_qkv, cotangent, out_weight, qkv_weight, offsets, sink_frame, window):
    frames_dev, strip_len, _ = cotangent.shape
    frames, spots, lines = frames_dev * n, strip_len // n, n // 4
    local = jnp.concatenate([out_weight[None], qkv_weight], axis=0)
    if strips > 2:
        groups = [list(range(strips // 2)), list(range(strips // 2, strips))]
        local = lax.all_gather(local, "strip", axis_index_groups=groups, axis=2, tiled=True)
    send = jnp.concatenate([saved_qkv, cotangent], axis=2).transpose(1, 0, 2)
    bias = jnp.where(visibility(offsets, sink_frame, window), 0.0, -jnp.inf).astype(jnp.float32)
    dma = pltpu.SemaphoreType.DMA
    returned = pl.pallas_call(
        functools.partial(block_kernel, n, strips, spots),
        out_shape=jax.ShapeDtypeStruct((strip_len, frames_dev, D), jnp.bfloat16),
        in_specs=[VMEM_SPEC] * 3,
        out_specs=VMEM_SPEC,
        scratch_shapes=[
            pltpu.VMEM((spots, n, frames_dev, 4 * D), jnp.bfloat16),
            pltpu.VMEM((2, 2, D // n, D // 2), jnp.bfloat16),
            pltpu.VMEM((4, n // 2, 2 * D // n, D), jnp.bfloat16),
            pltpu.VMEM((frames, 3 * D), jnp.bfloat16),
            pltpu.VMEM((frames, D), jnp.bfloat16),
            pltpu.VMEM((frames, 3 * D), jnp.float32),
            pltpu.VMEM((spots, n, frames_dev, D), jnp.bfloat16),
            dma((1 + 2 * spots,)),
            dma((4,)), dma((4,)),
            dma((lines,)), dma((lines,)),
            dma((lines,)), dma((lines,)),
            dma((2 * lines,)), dma((2 * lines,)),
            dma((2 * lines,)), dma((2 * lines,)),
            dma((2 * lines,)), dma((2 * lines,)),
            dma((spots, n)), dma((spots, n)),
            dma((spots, n)), dma((spots, n)),
        ],
        compiler_params=pltpu.CompilerParams(
            collective_id=0, has_side_effects=True, vmem_limit_bytes=48 << 20
        ),
        name="block",
    )(send, local, bias)
    return returned.transpose(1, 0, 2)


def solution(mesh):
    placed = (
        P("frame", "strip", None),
        P("frame", "strip", None),
        P("frame", "strip"),
        P(None, "frame", "strip"),
        P(),
        P(),
        P(),
    )
    return jax.shard_map(
        functools.partial(per_device, mesh.shape["frame"], mesh.shape["strip"]),
        mesh=mesh,
        in_specs=placed,
        out_specs=P("frame", "strip", None),
        check_vma=False,
    )
```

```python
import functools
import math

import jax
import jax.numpy as jnp
from jax import lax
from jax.experimental import pallas as pl
from jax.experimental.pallas import tpu as pltpu
from jax.sharding import PartitionSpec as P

D = 1152
H = 16
HD = 72
LANES = 128
GROUP = 4
MESH = pl.DeviceIdType.MESH
VMEM_SPEC = pl.BlockSpec(memory_space=pltpu.VMEM)


def visibility(offsets, sink_frame, window):
    frame_ids = jnp.arange(offsets.shape[0], dtype=jnp.int32)
    time_gap = offsets[:, None] - offsets[None, :]
    in_window = time_gap < window[0]
    anchor = frame_ids[None, :] == sink_frame[0]
    return (time_gap >= 0) & (in_window | anchor)


def remote(src, dst, send_sem, recv_sem, to):
    return pltpu.make_async_remote_copy(
        src_ref=src, dst_ref=dst, send_sem=send_sem, recv_sem=recv_sem,
        device_id=to, device_id_type=MESH,
    )


def nt_dot(a, b):
    return lax.dot_general(a, b, (((1,), (1,)), ((), ())), preferred_element_type=jnp.float32)


def head_columns(h):
    low = h * HD // LANES * LANES
    high = -(-(h * HD + HD) // LANES) * LANES
    return low, high


def heads_gradients(x_ref, grad_out, bias, grads):
    factor = 1.0 / math.sqrt(HD)
    frames = bias.shape[0]
    grads[...] = jnp.zeros_like(grads)

    def part(ref, start, h, masked=True):
        low, high = head_columns(h)
        rows = ref[:, start + low : start + high]
        if not masked:
            return rows
        feature = lax.broadcasted_iota(jnp.int32, rows.shape, 1) + low
        own = (feature >= h * HD) & (feature < h * HD + HD)
        return jnp.where(own, rows, jnp.zeros_like(rows))

    def plain_dot(a, b):
        return jnp.dot(a, b, preferred_element_type=jnp.float32)

    for first in range(0, H, GROUP):
        heads = range(first, first + GROUP)
        scores = [nt_dot(part(x_ref, 0, h), part(x_ref, D, h, False)) for h in heads]
        grad_p = [nt_dot(part(grad_out, 0, h), part(x_ref, 2 * D, h, False)) for h in heads]
        scores = [one * factor + bias for one in scores]
        tops = [jnp.max(one, axis=1, keepdims=True) for one in scores]
        raised = [jnp.exp(one - top) for one, top in zip(scores, tops)]
        sums = [jnp.sum(one, axis=1, keepdims=True) for one in raised]
        probs = [one * (1.0 / total) for one, total in zip(raised, sums)]
        probs_t = [one.T.astype(jnp.bfloat16) for one in probs]
        row_sums = [jnp.sum(p * gp, axis=1, keepdims=True) for p, gp in zip(probs, grad_p)]
        grad_s = [p * (gp - rs) for p, gp, rs in zip(probs, grad_p, row_sums)]
        grad_s_t = [one.T.astype(jnp.bfloat16) for one in grad_s]
        grad_s = [one.astype(jnp.bfloat16) for one in grad_s]
        grad_v = [plain_dot(p, part(grad_out, 0, h)) for p, h in zip(probs_t, heads)]
        grad_q = [plain_dot(gs, part(x_ref, D, h)) * factor for gs, h in zip(grad_s, heads)]
        grad_k = [plain_dot(gs, part(x_ref, 0, h)) * factor for gs, h in zip(grad_s_t, heads)]
        for h, gq, gk, gv in zip(heads, grad_q, grad_k, grad_v):
            low, high = head_columns(h)
            grads[:, low:high] += gq
            grads[:, D + low : D + high] += gk
            grads[:, 2 * D + low : 2 * D + high] += gv


def block_kernel(
    n, strips, spots, send_ref, local_ref, bias_ref, ret_ref,
    recv, pieces, weights, xs, grad_out, grads, outs,
    own_sem, piece_send, piece_recv, z_send, z_recv, y_send, y_recv,
    x_send, x_recv, mine_send, mine_recv, other_send, other_recv,
    in_send, in_recv, out_send, out_recv,
):
    frames = bias_ref.shape[0]
    lines = n // 4
    me, strip = lax.axis_index("frame"), lax.axis_index("strip")
    half, x, y, z = strip // (strips // 2), lax.rem(me, 2), lax.rem(me // 2, 2), me // 4
    twin = lax.rem(strip + strips // 2, strips)
    beside = me + 1 - 2 * x
    matrix = 2 * half + x

    barrier = pltpu.get_barrier_semaphore()

    @pl.loop(1, n)
    def _(d):
        pl.semaphore_signal(
            barrier, inc=1, device_id=(lax.rem(me + d, n), strip), device_id_type=MESH
        )

    for to in ((me, twin), (beside, twin)):
        pl.semaphore_signal(barrier, inc=1, device_id=to, device_id_type=MESH)
    pl.semaphore_wait(barrier, n + 1)

    def piece(k):
        to_x, to_half = lax.rem(x + k // 2, 2), lax.rem(half + k % 2, 2)
        return remote(
            local_ref.at[2 * to_half + to_x], pieces.at[x, half],
            piece_send.at[k], piece_recv.at[k],
            (beside if k // 2 else me, twin if k % 2 else strip),
        )

    for k in (1, 2, 3):
        piece(k).start()
    own = pltpu.make_async_copy(local_ref.at[matrix], pieces.at[x, half], own_sem.at[0])
    own.start()

    def inward(j, d):
        to = lax.rem(me + d, n)
        return remote(
            send_ref.at[to * spots + j], recv.at[j, me],
            in_send.at[j, d], in_recv.at[j, d], (to, strip),
        )

    def own_inward(j):
        return pltpu.make_async_copy(
            send_ref.at[me * spots + j], recv.at[j, me], own_sem.at[1 + j]
        )

    def start_inward(j):
        @pl.loop(1, n)
        def _(d):
            inward(j, d).start()

        own_inward(j).start()

    own.wait()
    for k in (1, 2, 3):
        piece(k).wait()
    rows = [
        jnp.concatenate([pieces[i, c].astype(jnp.float32) for c in range(2)], axis=1)
        for i in range(2)
    ]
    weights[matrix, 2 * z + y] = jnp.concatenate(rows, axis=0).astype(jnp.bfloat16)

    def block_at(k):
        return 2 * lax.rem(z + lines - k % lines, lines) + lax.rem(y + k // lines, 2)

    def along_z(d):
        to = 4 * lax.rem(z + d, lines) + lax.rem(me, 4)
        ref = weights.at[matrix, 2 * z + y]
        return remote(ref, ref, z_send.at[d], z_recv.at[d], (to, strip))

    def across_y(k):
        ref = weights.at[matrix, block_at(k)]
        return remote(ref, ref, y_send.at[k], y_recv.at[k], (me + 2 - 4 * y, strip))

    def across_x(k):
        ref = weights.at[matrix, block_at(k)]
        return remote(ref, ref, x_send.at[k], x_recv.at[k], (beside, strip))

    def mine_to_twin(k):
        ref = weights.at[matrix, block_at(k)]
        return remote(ref, ref, mine_send.at[k], mine_recv.at[k], (me, twin))

    def other_to_twin(k):
        ref = weights.at[2 * half + 1 - x, block_at(k)]
        return remote(ref, ref, other_send.at[k], other_recv.at[k], (me, twin))

    @pl.loop(1, lines)
    def _(d):
        along_z(d).start()

    across_y(0).start()
    across_x(0).start()
    mine_to_twin(0).start()
    start_inward(0)

    @pl.loop(1, lines)
    def _(k):
        along_z(k).wait_recv()
        across_y(k).start()
        across_x(k).start()
        mine_to_twin(k).start()

    start_inward(1)

    @pl.loop(0, lines)
    def _(k):
        across_y(k).wait_recv()
        across_x(k + lines).start()
        mine_to_twin(k + lines).start()

    for j in range(2, spots):
        start_inward(j)

    @pl.loop(0, 2 * lines)
    def _(k):
        across_x(k).wait_recv()
        other_to_twin(k).start()

    @pl.loop(0, 2 * lines)
    def _(k):
        mine_to_twin(k).wait()
        other_to_twin(k).wait()
        across_x(k).wait_send()

    @pl.loop(1, lines)
    def _(d):
        along_z(d).wait_send()

    @pl.loop(0, lines)
    def _(k):
        across_y(k).wait_send()

    def outward(j, d):
        to = lax.rem(me + d, n)
        return remote(
            outs.at[j, to], ret_ref.at[me * spots + j],
            out_send.at[j, d], out_recv.at[j, d], (to, strip),
        )

    def own_outward(j):
        return pltpu.make_async_copy(
            outs.at[j, me], ret_ref.at[me * spots + j], own_sem.at[1 + spots + j]
        )

    def whole(m):
        return weights[m].reshape(D, D)

    @pl.loop(0, spots)
    def _(j):
        own_inward(j).wait()

        @pl.loop(1, n)
        def _(d):
            inward(j, d).wait()

        moved = recv[j].astype(jnp.float32).reshape(frames, 4 * D).astype(jnp.bfloat16)
        xs[...] = moved[:, : 3 * D]
        grad_out[...] = nt_dot(moved[:, 3 * D :], whole(0)).astype(jnp.bfloat16)
        heads_gradients(xs, grad_out, bias_ref[...], grads)
        total = nt_dot(grads[:, :D].astype(jnp.bfloat16), whole(1))
        total += nt_dot(grads[:, D : 2 * D].astype(jnp.bfloat16), whole(2))
        total += nt_dot(grads[:, 2 * D :].astype(jnp.bfloat16), whole(3))
        outs[j] = total.reshape(n, frames // n, D).astype(jnp.bfloat16)

        @pl.loop(1, n)
        def _(d):
            outward(j, d).start()

        own_outward(j).start()

    @pl.loop(0, spots)
    def _(j):
        own_outward(j).wait()

        @pl.loop(1, n)
        def _(d):
            outward(j, d).wait()


def per_device(n, strips, saved_qkv, cotangent, out_weight, qkv_weight, offsets, sink_frame, window):
    frames_dev, strip_len, _ = cotangent.shape
    frames, spots, lines = frames_dev * n, strip_len // n, n // 4
    local = jnp.concatenate([out_weight[None], qkv_weight], axis=0)
    if strips > 2:
        groups = [list(range(strips // 2)), list(range(strips // 2, strips))]
        local = lax.all_gather(local, "strip", axis_index_groups=groups, axis=2, tiled=True)
    send = jnp.concatenate([saved_qkv, cotangent], axis=2).transpose(1, 0, 2)
    bias = jnp.where(visibility(offsets, sink_frame, window), 0.0, -jnp.inf).astype(jnp.float32)
    dma = pltpu.SemaphoreType.DMA
    returned = pl.pallas_call(
        functools.partial(block_kernel, n, strips, spots),
        out_shape=jax.ShapeDtypeStruct((strip_len, frames_dev, D), jnp.bfloat16),
        in_specs=[VMEM_SPEC] * 3,
        out_specs=VMEM_SPEC,
        scratch_shapes=[
            pltpu.VMEM((spots, n, frames_dev, 4 * D), jnp.bfloat16),
            pltpu.VMEM((2, 2, D // n, D // 2), jnp.bfloat16),
            pltpu.VMEM((4, n // 2, 2 * D // n, D), jnp.bfloat16),
            pltpu.VMEM((frames, 3 * D), jnp.bfloat16),
            pltpu.VMEM((frames, D), jnp.bfloat16),
            pltpu.VMEM((frames, 3 * D), jnp.float32),
            pltpu.VMEM((spots, n, frames_dev, D), jnp.bfloat16),
            dma((1 + 2 * spots,)),
            dma((4,)), dma((4,)),
            dma((lines,)), dma((lines,)),
            dma((lines,)), dma((lines,)),
            dma((2 * lines,)), dma((2 * lines,)),
            dma((2 * lines,)), dma((2 * lines,)),
            dma((2 * lines,)), dma((2 * lines,)),
            dma((spots, n)), dma((spots, n)),
            dma((spots, n)), dma((spots, n)),
        ],
        compiler_params=pltpu.CompilerParams(
            collective_id=0, has_side_effects=True, vmem_limit_bytes=48 << 20
        ),
        name="block",
    )(send, local, bias)
    return returned.transpose(1, 0, 2)


def solution(mesh):
    placed = (
        P("frame", "strip", None),
        P("frame", "strip", None),
        P("frame", "strip"),
        P(None, "frame", "strip"),
        P(),
        P(),
        P(),
    )
    return jax.shard_map(
        functools.partial(per_device, mesh.shape["frame"], mesh.shape["strip"]),
        mesh=mesh,
        in_specs=placed,
        out_specs=P("frame", "strip", None),
        check_vma=False,
    )
```

```python
import functools
import math

import jax
import jax.numpy as jnp
from jax import lax
from jax.experimental import pallas as pl
from jax.experimental.pallas import tpu as pltpu
from jax.sharding import PartitionSpec as P

D = 1152
H = 16
HD = 72
LANES = 128
GROUP = 4
MESH = pl.DeviceIdType.MESH
VMEM_SPEC = pl.BlockSpec(memory_space=pltpu.VMEM)


def visibility(offsets, sink_frame, window):
    frame_ids = jnp.arange(offsets.shape[0], dtype=jnp.int32)
    time_gap = offsets[:, None] - offsets[None, :]
    in_window = time_gap < window[0]
    anchor = frame_ids[None, :] == sink_frame[0]
    return (time_gap >= 0) & (in_window | anchor)


def remote(src, dst, send_sem, recv_sem, to):
    return pltpu.make_async_remote_copy(
        src_ref=src, dst_ref=dst, send_sem=send_sem, recv_sem=recv_sem,
        device_id=to, device_id_type=MESH,
    )


def nt_dot(a, b):
    return lax.dot_general(a, b, (((1,), (1,)), ((), ())), preferred_element_type=jnp.float32)


def head_columns(h):
    low = h * HD // LANES * LANES
    high = -(-(h * HD + HD) // LANES) * LANES
    return low, high


def heads_gradients(x_ref, grad_out, bias, grads):
    factor = 1.0 / math.sqrt(HD)
    frames = bias.shape[0]
    grads[...] = jnp.zeros_like(grads)

    def part(ref, start, h, masked=True):
        low, high = head_columns(h)
        rows = ref[:, start + low : start + high]
        if not masked:
            return rows
        feature = lax.broadcasted_iota(jnp.int32, rows.shape, 1) + low
        own = (feature >= h * HD) & (feature < h * HD + HD)
        return jnp.where(own, rows, jnp.zeros_like(rows))

    def plain_dot(a, b):
        return jnp.dot(a, b, preferred_element_type=jnp.float32)

    for first in range(0, H, GROUP):
        heads = range(first, first + GROUP)
        scores = [nt_dot(part(x_ref, 0, h), part(x_ref, D, h, False)) for h in heads]
        grad_p = [nt_dot(part(grad_out, 0, h), part(x_ref, 2 * D, h, False)) for h in heads]
        scores = [one * factor + bias for one in scores]
        tops = [jnp.max(one, axis=1, keepdims=True) for one in scores]
        raised = [jnp.exp(one - top) for one, top in zip(scores, tops)]
        sums = [jnp.sum(one, axis=1, keepdims=True) for one in raised]
        probs = [one * (1.0 / total) for one, total in zip(raised, sums)]
        probs_t = [one.T.astype(jnp.bfloat16) for one in probs]
        row_sums = [jnp.sum(p * gp, axis=1, keepdims=True) for p, gp in zip(probs, grad_p)]
        grad_s = [p * (gp - rs) for p, gp, rs in zip(probs, grad_p, row_sums)]
        grad_s_t = [one.T.astype(jnp.bfloat16) for one in grad_s]
        grad_s = [one.astype(jnp.bfloat16) for one in grad_s]
        grad_v = [plain_dot(p, part(grad_out, 0, h)) for p, h in zip(probs_t, heads)]
        grad_q = [plain_dot(gs, part(x_ref, D, h)) * factor for gs, h in zip(grad_s, heads)]
        grad_k = [plain_dot(gs, part(x_ref, 0, h)) * factor for gs, h in zip(grad_s_t, heads)]
        for h, gq, gk, gv in zip(heads, grad_q, grad_k, grad_v):
            low, high = head_columns(h)
            grads[:, low:high] += gq
            grads[:, D + low : D + high] += gk
            grads[:, 2 * D + low : 2 * D + high] += gv


def block_kernel(
    n, strips, spots, send_ref, local_ref, bias_ref, ret_ref,
    recv, pieces, weights, xs, grad_out, grads, outs,
    own_sem, piece_send, piece_recv, z_send, z_recv, y_send, y_recv,
    x_send, x_recv, mine_send, mine_recv, other_send, other_recv,
    in_send, in_recv, out_send, out_recv,
):
    frames = bias_ref.shape[0]
    lines = n // 4
    me, strip = lax.axis_index("frame"), lax.axis_index("strip")
    half, x, y, z = strip // (strips // 2), lax.rem(me, 2), lax.rem(me // 2, 2), me // 4
    twin = lax.rem(strip + strips // 2, strips)
    beside = me + 1 - 2 * x
    matrix = 2 * half + x

    barrier = pltpu.get_barrier_semaphore()

    @pl.loop(1, n)
    def _(d):
        pl.semaphore_signal(
            barrier, inc=1, device_id=(lax.rem(me + d, n), strip), device_id_type=MESH
        )

    for to in ((me, twin), (beside, twin)):
        pl.semaphore_signal(barrier, inc=1, device_id=to, device_id_type=MESH)
    pl.semaphore_wait(barrier, n + 1)

    def piece(k):
        to_x, to_half = lax.rem(x + k // 2, 2), lax.rem(half + k % 2, 2)
        return remote(
            local_ref.at[2 * to_half + to_x], pieces.at[x, half],
            piece_send.at[k], piece_recv.at[k],
            (beside if k // 2 else me, twin if k % 2 else strip),
        )

    for k in (1, 2, 3):
        piece(k).start()
    own = pltpu.make_async_copy(local_ref.at[matrix], pieces.at[x, half], own_sem.at[0])
    own.start()

    def inward(j, d):
        to = lax.rem(me + d, n)
        return remote(
            send_ref.at[to * spots + j], recv.at[j, me],
            in_send.at[j, d], in_recv.at[j, d], (to, strip),
        )

    def own_inward(j):
        return pltpu.make_async_copy(
            send_ref.at[me * spots + j], recv.at[j, me], own_sem.at[1 + j]
        )

    def start_inward(j):
        @pl.loop(1, n)
        def _(d):
            inward(j, d).start()

        own_inward(j).start()

    own.wait()
    for k in (1, 2, 3):
        piece(k).wait()
    rows = [
        jnp.concatenate([pieces[i, c].astype(jnp.float32) for c in range(2)], axis=1)
        for i in range(2)
    ]
    weights[matrix, 2 * z + y] = jnp.concatenate(rows, axis=0).astype(jnp.bfloat16)

    def block_at(k):
        return 2 * lax.rem(z + lines - k % lines, lines) + lax.rem(y + k // lines, 2)

    def along_z(d):
        to = 4 * lax.rem(z + d, lines) + lax.rem(me, 4)
        ref = weights.at[matrix, 2 * z + y]
        return remote(ref, ref, z_send.at[d], z_recv.at[d], (to, strip))

    def across_y(k):
        ref = weights.at[matrix, block_at(k)]
        return remote(ref, ref, y_send.at[k], y_recv.at[k], (me + 2 - 4 * y, strip))

    def across_x(k):
        ref = weights.at[matrix, block_at(k)]
        return remote(ref, ref, x_send.at[k], x_recv.at[k], (beside, strip))

    def mine_to_twin(k):
        ref = weights.at[matrix, block_at(k)]
        return remote(ref, ref, mine_send.at[k], mine_recv.at[k], (me, twin))

    def other_to_twin(k):
        ref = weights.at[2 * half + 1 - x, block_at(k)]
        return remote(ref, ref, other_send.at[k], other_recv.at[k], (me, twin))

    @pl.loop(1, lines)
    def _(d):
        along_z(d).start()

    across_y(0).start()
    across_x(0).start()
    mine_to_twin(0).start()
    for j in range(spots):
        start_inward(j)

    @pl.loop(1, lines)
    def _(k):
        along_z(k).wait_recv()
        across_y(k).start()
        across_x(k).start()
        mine_to_twin(k).start()

    @pl.loop(0, lines)
    def _(k):
        across_y(k).wait_recv()
        across_x(k + lines).start()
        mine_to_twin(k + lines).start()

    @pl.loop(0, 2 * lines)
    def _(k):
        across_x(k).wait_recv()
        other_to_twin(k).start()

    @pl.loop(0, 2 * lines)
    def _(k):
        mine_to_twin(k).wait()
        other_to_twin(k).wait()
        across_x(k).wait_send()

    @pl.loop(1, lines)
    def _(d):
        along_z(d).wait_send()

    @pl.loop(0, lines)
    def _(k):
        across_y(k).wait_send()

    def outward(j, d):
        to = lax.rem(me + d, n)
        return remote(
            outs.at[j, to], ret_ref.at[me * spots + j],
            out_send.at[j, d], out_recv.at[j, d], (to, strip),
        )

    def own_outward(j):
        return pltpu.make_async_copy(
            outs.at[j, me], ret_ref.at[me * spots + j], own_sem.at[1 + spots + j]
        )

    def whole(m):
        return weights[m].reshape(D, D)

    @pl.loop(0, spots)
    def _(j):
        own_inward(j).wait()

        @pl.loop(1, n)
        def _(d):
            inward(j, d).wait()

        moved = recv[j].astype(jnp.float32).reshape(frames, 4 * D).astype(jnp.bfloat16)
        xs[...] = moved[:, : 3 * D]
        grad_out[...] = nt_dot(moved[:, 3 * D :], whole(0)).astype(jnp.bfloat16)
        heads_gradients(xs, grad_out, bias_ref[...], grads)
        total = nt_dot(grads[:, :D].astype(jnp.bfloat16), whole(1))
        total += nt_dot(grads[:, D : 2 * D].astype(jnp.bfloat16), whole(2))
        total += nt_dot(grads[:, 2 * D :].astype(jnp.bfloat16), whole(3))
        outs[j] = total.reshape(n, frames // n, D).astype(jnp.bfloat16)

        @pl.loop(1, n)
        def _(d):
            outward(j, d).start()

        own_outward(j).start()

    @pl.loop(0, spots)
    def _(j):
        own_outward(j).wait()

        @pl.loop(1, n)
        def _(d):
            outward(j, d).wait()


def per_device(n, strips, saved_qkv, cotangent, out_weight, qkv_weight, offsets, sink_frame, window):
    frames_dev, strip_len, _ = cotangent.shape
    frames, spots, lines = frames_dev * n, strip_len // n, n // 4
    local = jnp.concatenate([out_weight[None], qkv_weight], axis=0)
    if strips > 2:
        groups = [list(range(strips // 2)), list(range(strips // 2, strips))]
        local = lax.all_gather(local, "strip", axis_index_groups=groups, axis=2, tiled=True)
    send = jnp.concatenate([saved_qkv, cotangent], axis=2).transpose(1, 0, 2)
    bias = jnp.where(visibility(offsets, sink_frame, window), 0.0, -jnp.inf).astype(jnp.float32)
    dma = pltpu.SemaphoreType.DMA
    returned = pl.pallas_call(
        functools.partial(block_kernel, n, strips, spots),
        out_shape=jax.ShapeDtypeStruct((strip_len, frames_dev, D), jnp.bfloat16),
        in_specs=[VMEM_SPEC] * 3,
        out_specs=VMEM_SPEC,
        scratch_shapes=[
            pltpu.VMEM((spots, n, frames_dev, 4 * D), jnp.bfloat16),
            pltpu.VMEM((2, 2, D // n, D // 2), jnp.bfloat16),
            pltpu.VMEM((4, n // 2, 2 * D // n, D), jnp.bfloat16),
            pltpu.VMEM((frames, 3 * D), jnp.bfloat16),
            pltpu.VMEM((frames, D), jnp.bfloat16),
            pltpu.VMEM((frames, 3 * D), jnp.float32),
            pltpu.VMEM((spots, n, frames_dev, D), jnp.bfloat16),
            dma((1 + 2 * spots,)),
            dma((4,)), dma((4,)),
            dma((lines,)), dma((lines,)),
            dma((lines,)), dma((lines,)),
            dma((2 * lines,)), dma((2 * lines,)),
            dma((2 * lines,)), dma((2 * lines,)),
            dma((2 * lines,)), dma((2 * lines,)),
            dma((spots, n)), dma((spots, n)),
            dma((spots, n)), dma((spots, n)),
        ],
        compiler_params=pltpu.CompilerParams(
            collective_id=0, has_side_effects=True, vmem_limit_bytes=48 << 20
        ),
        name="block",
    )(send, local, bias)
    return returned.transpose(1, 0, 2)


def solution(mesh):
    placed = (
        P("frame", "strip", None),
        P("frame", "strip", None),
        P("frame", "strip"),
        P(None, "frame", "strip"),
        P(),
        P(),
        P(),
    )
    return jax.shard_map(
        functools.partial(per_device, mesh.shape["frame"], mesh.shape["strip"]),
        mesh=mesh,
        in_specs=placed,
        out_specs=P("frame", "strip", None),
        check_vma=False,
    )
```
